32 devices in a mesh: neuron: 4 (over z), tm: 2 (over core), trial: 4 (over y, x).
Axes of the slice: x: 2, y: 2, z: 4, core: 2. Of those that a mesh axis runs over, the one named last changes fastest.
Arguments:
- tensor: bfloat16 [1024, 256, 512], P('neuron', 'tm', 'trial'), may hold values from -6 to 6
- present_blocks: int32 [8, 16], P('neuron'), may hold values 0 or 1
- trial_day: int32 [512], P('trial'), may hold values from 0 to 15
- time_factor: bfloat16 [256, 256], P('tm'), may hold values from 0 to 1
- trial_factor: bfloat16 [512, 256], P('trial'), may hold values from 0 to 1
Outputs:
- neuron_out: bfloat16 [1024, 256], P(('neuron', 'tm', 'trial'))
- time_out: bfloat16 [256, 256], P('tm')
- trial_out: bfloat16 [512, 256], P('trial')
The draws below stay inside these ranges and needn't reach their ends.
All inputs are finite; a program needn't handle non-finite values. No bound on the sum of `present_blocks` on one device may be relied on, other than what follows from the above.
Results may differ from the reference program's by a relative error of at most 0.0051.
The reference program's roundings to bfloat16 on the way count: a program that leaves them out, or rounds other values in their place, can miss the bound.
Values may be sent and summed in bfloat16 or wider, within the bound.
A program may use at most 128 MiB of HBM per device.

```python
import jax
import jax.numpy as jnp
from jax import lax

R = 256
BLOCK = 128
DAYS = 16
NBLK = 8
NEU = 1024
TIME = 256
TRIALS = 512


def touch_ends(entries, own_key, smallest, largest):
    longest = entries.shape.index(max(entries.shape))
    spots = []
    for shift in (0, 1):
        where = [jax.random.randint(jax.random.fold_in(own_key, axis), (), 0, length) for axis, length in enumerate(entries.shape)]
        where[longest] = (where[longest] + shift) % entries.shape[longest]
        spots.append(tuple(where))
    return entries.at[spots[0]].set(smallest).at[spots[1]].set(largest)


def with_spikes(drawn, own_key, source, target, parts, factor):
    def block_of(dim):
        return (jnp.arange(drawn.shape[dim]) // (drawn.shape[dim] // parts)).reshape((-1,) + (1,) * (drawn.ndim - 1 - dim))

    near = jax.random.permutation(own_key, parts)[block_of(target)]
    second = (block_of(target) + parts // 2) % parts
    return jnp.where((block_of(source) == near) | (block_of(source) == second), factor * drawn, drawn)


def levels(own_key, shape, pieces, low, largest):
    def one(position, parts):
        steps = jax.random.uniform(jax.random.fold_in(jax.random.fold_in(own_key, 6), position), (parts,), jnp.float32, low / len(pieces), largest / len(pieces))
        return jnp.repeat(jnp.exp(steps), shape[position] // parts).reshape((-1,) + (1,) * (len(shape) - position - 1))

    factor_of = one(*pieces[0])
    for cut in pieces[1:]:
        factor_of = factor_of * one(*cut)
    return factor_of


def gaussian_with(rng, dims, width, bound, split, heavy, kind=jnp.bfloat16):
    drawn = width * jax.random.normal(rng, dims, jnp.float32)
    if split:
        drawn = drawn * levels(rng, dims, split, -0.22, 0.18)
    return jnp.clip(with_spikes(drawn, jax.random.fold_in(rng, 3), *heavy), -bound, bound).astype(kind)


def setup_inputs(seed: int = 0) -> dict:
    key_of = jax.random.split(jax.random.key(seed), 6)
    return {
        "tensor": gaussian_with(key_of[0], (NEU, TIME, TRIALS), 1.0, 6.0, ((0, 4), (1, 2), (2, 4)), (0, 1, 4, 2.0)),
        "present_blocks": touch_ends((jax.random.randint(key_of[1], (NBLK, DAYS), 0, 4) < 3).astype(jnp.int32), jax.random.fold_in(key_of[1], 1), 0, 1),
        "trial_day": touch_ends(jax.random.randint(key_of[2], (TRIALS,), 0, DAYS), jax.random.fold_in(key_of[2], 1), 0, DAYS - 1).astype(jnp.int32),
        "time_factor": jnp.clip(1.0 * jax.random.uniform(key_of[3], (TIME, R), jnp.float32) ** levels(key_of[3], (TIME, R), ((0, 2),), -0.2, 0.2), 0.0, 1.0).astype(jnp.bfloat16),
        "trial_factor": jnp.clip(1.0 * jax.random.uniform(key_of[4], (TRIALS, R), jnp.float32) ** levels(key_of[4], (TRIALS, R), ((0, 4),), -0.2, 0.2), 0.0, 1.0).astype(jnp.bfloat16),
    }


RIDGE = 0.1
EPSILON = 1e-06

def normal_inverse(gram_matrix):
    order_size = gram_matrix.shape[0]
    identity = jnp.eye(order_size, dtype=jnp.float32)
    scaled = gram_matrix / jnp.mean(jnp.diagonal(gram_matrix)) + RIDGE * identity
    lower_factor = jnp.linalg.cholesky(scaled)
    return jax.scipy.linalg.cho_solve((lower_factor, True), identity)

def khatri_rao(left_rows, right_rows):
    return (left_rows.astype(jnp.float32)[:, None, :] * right_rows.astype(jnp.float32)[None, :, :]).astype(jnp.bfloat16)

def rescale(raw_rows, total_rows):
    gram_raw = jnp.dot(raw_rows.T, raw_rows, precision=lax.Precision.HIGHEST)
    scales = jnp.sqrt(jnp.diagonal(gram_raw) / total_rows + EPSILON)
    factor = (raw_rows / scales[None, :]).astype(jnp.bfloat16)
    normed = gram_raw / (scales[:, None] * scales[None, :])
    return (factor, normed)

def reference(tensor, present_blocks, trial_day, time_factor, trial_factor):
    block_mask = present_blocks[:, trial_day].astype(jnp.float32)
    tensor_blocks = tensor.reshape(NBLK, BLOCK, TIME, TRIALS)
    gram_time = jnp.dot(time_factor.T.astype(jnp.float32), time_factor.astype(jnp.float32), preferred_element_type=jnp.float32)
    gram_trial = jnp.dot(trial_factor.T.astype(jnp.float32), trial_factor.astype(jnp.float32), preferred_element_type=jnp.float32)
    kr_tk = khatri_rao(time_factor, trial_factor).astype(jnp.float32)

    def neuron_block(inputs):
        tensor_piece, mask_row = inputs
        masked = tensor_piece.astype(jnp.float32) * mask_row[None, None, :]
        return jnp.einsum('itk,tkr->ir', masked, kr_tk, precision=lax.Precision.HIGHEST)
    mttkrp_neuron = lax.map(neuron_block, (tensor_blocks, block_mask)).reshape(NEU, R)
    raw_neuron = jnp.dot(mttkrp_neuron, normal_inverse(gram_time * gram_trial), precision=lax.Precision.HIGHEST)
    neuron_out, gram_neuron = rescale(raw_neuron, NEU)
    neuron_blocks = neuron_out.reshape(NBLK, BLOCK, R)

    def time_block(running, inputs):
        tensor_piece, mask_row, rows_a = inputs
        masked = tensor_piece.astype(jnp.float32) * mask_row[None, None, :]
        kr_ik = khatri_rao(rows_a, trial_factor).astype(jnp.float32)
        return (running + jnp.einsum('itk,ikr->tr', masked, kr_ik, precision=lax.Precision.HIGHEST), None)
    mttkrp_time, unused = lax.scan(time_block, jnp.zeros((TIME, R), jnp.float32), (tensor_blocks, block_mask, neuron_blocks))
    raw_time = jnp.dot(mttkrp_time, normal_inverse(gram_neuron * gram_trial), precision=lax.Precision.HIGHEST)
    time_out, gram_time_new = rescale(raw_time, TIME)

    def trial_block(running, inputs):
        tensor_piece, mask_row, rows_a = inputs
        masked = tensor_piece.astype(jnp.float32) * mask_row[None, None, :]
        kr_it = khatri_rao(rows_a, time_out).astype(jnp.float32)
        return (running + jnp.einsum('itk,itr->kr', masked, kr_it, precision=lax.Precision.HIGHEST), None)
    mttkrp_trial, unused = lax.scan(trial_block, jnp.zeros((TRIALS, R), jnp.float32), (tensor_blocks, block_mask, neuron_blocks))
    raw_trial = jnp.dot(mttkrp_trial, normal_inverse(gram_neuron * gram_time_new), precision=lax.Precision.HIGHEST)
    scales = jnp.sqrt(lax.optimization_barrier(jnp.sum(raw_trial * raw_trial, axis=0)) / TRIALS + EPSILON)
    trial_out = (raw_trial / scales[None, :]).astype(jnp.bfloat16)
    return (neuron_out, time_out, trial_out)
```

```python
import functools

import jax
import jax.numpy as jnp
from jax import lax
from jax.experimental import pallas as pl
from jax.experimental.pallas import tpu as pltpu
from jax.sharding import PartitionSpec as P

RIDGE = 0.1
EPSILON = 1e-06
PANEL = 4
VMEM = pl.BlockSpec(memory_space=pltpu.VMEM)
F32 = jnp.float32
BF16 = jnp.bfloat16
TN = (((0,), (0,)), ((), ()))


def dot_high(left, right):
    return jnp.dot(left, right, precision=lax.Precision.HIGHEST, preferred_element_type=F32)


def gram_high(rows):
    return lax.dot_general(
        rows, rows, TN, precision=lax.Precision.HIGHEST, preferred_element_type=F32
    )


def diagonals(square):
    size = square.shape[0]
    on = lax.broadcasted_iota(jnp.int32, (size, size), 0) == lax.broadcasted_iota(
        jnp.int32, (size, size), 1
    )
    kept = jnp.where(on, square, 0.0)
    return jnp.sum(kept, axis=0, keepdims=True), jnp.sum(kept, axis=1, keepdims=True)


class Group:
    def __init__(self, axes, sizes):
        self.axes = axes
        self.sizes = [sizes[axis] for axis in axes]
        self.count = 1
        for size in self.sizes:
            self.count *= size

    def me(self):
        index = 0
        for axis, size in zip(self.axes, self.sizes):
            index = index * size + lax.axis_index(axis)
        return index

    def where(self, index):
        place = {}
        for axis, size in reversed(list(zip(self.axes, self.sizes))):
            place[axis] = lax.rem(index, size)
            index = index // size
        return place

    def each(self, body):
        if self.count <= 32:
            for step in range(1, self.count):
                body(step)
        else:

            @pl.loop(1, self.count)
            def run(step):
                body(step)

    def greet(self, barrier):
        me = self.me()

        def body(step):
            pl.semaphore_signal(
                barrier,
                inc=1,
                device_id=self.where(lax.rem(me + step, self.count)),
                device_id_type=pl.DeviceIdType.MESH,
            )

        self.each(body)

    def copy(self, step, source, target, sems, incoming):
        me = self.me()
        peer = lax.rem(me + step, self.count)
        origin = lax.rem(me - step + self.count, self.count)
        return pltpu.make_async_remote_copy(
            src_ref=source(peer),
            dst_ref=target(origin if incoming else me),
            send_sem=sems[0].at[step],
            recv_sem=sems[1].at[step],
            device_id=self.where(peer),
            device_id_type=pl.DeviceIdType.MESH,
        )

    def send(self, source, target, sems):
        self.each(lambda step: self.copy(step, source, target, sems, False).start())

    def wait(self, source, target, sems):
        self.each(lambda step: self.copy(step, source, target, sems, True).wait_recv())

    def flush(self, source, target, sems):
        self.each(lambda step: self.copy(step, source, target, sems, False).wait_send())

    def sems(self):
        return [pltpu.SemaphoreType.DMA((self.count,)), pltpu.SemaphoreType.DMA((self.count,))]


def meet(*groups):
    barrier = pltpu.get_barrier_semaphore()
    for group in groups:
        group.greet(barrier)
    pl.semaphore_wait(barrier, sum(group.count - 1 for group in groups))


def call(body, outs, scratch, number, *operands):
    return pl.pallas_call(
        body,
        out_shape=outs,
        in_specs=[VMEM] * len(operands),
        out_specs=[VMEM] * len(outs),
        scratch_shapes=scratch,
        compiler_params=pltpu.CompilerParams(
            collective_id=number, has_side_effects=True, vmem_limit_bytes=32 << 20
        ),
    )(*operands)


def summed(group, own_ref, landed_ref):
    me = group.me()
    landed_ref[me] = own_ref[me]
    if group.count <= 32:
        total = landed_ref[0]
        for index in range(1, group.count):
            total = total + landed_ref[index]
        return total
    return lax.fori_loop(
        1, group.count, lambda index, total: total + landed_ref[index], landed_ref[0]
    )


def start_kernel(by_time, by_trial, time_ref, trial_ref, gram_ref, product_ref, times, trials, ta, tb, ra, rb):
    meet(by_time, by_trial)
    jobs = (
        (by_trial, trial_ref, trials, (ra, rb)),
        (by_time, time_ref, times, (ta, tb)),
    )
    for group, own, landed, sems in jobs:
        group.send(lambda peer: own, lambda index: landed.at[index], sems)
    for group, own, landed, sems in jobs:
        landed[group.me()] = own[...]
        group.wait(lambda peer: own, lambda index: landed.at[index], sems)
    grams = []
    for landed in (times, trials):
        count, rows, rank = landed.shape
        whole = landed[...].reshape(count * rows, rank)
        grams.append(lax.dot_general(whole, whole, TN, preferred_element_type=F32))
    gram_ref[...] = grams[1]
    product_ref[...] = grams[0] * grams[1]
    for group, own, landed, sems in jobs:
        group.flush(lambda peer: own, lambda index: landed.at[index], sems)


def start_products(sizes, time_factor, trial_factor):
    by_time, by_trial = Group(("tm",), sizes), Group(("trial",), sizes)
    rank = time_factor.shape[1]
    square = jax.ShapeDtypeStruct((rank, rank), F32)
    return call(
        functools.partial(start_kernel, by_time, by_trial),
        [square, square],
        [
            pltpu.VMEM((by_time.count, *time_factor.shape), BF16),
            pltpu.VMEM((by_trial.count, *trial_factor.shape), BF16),
            *by_time.sems(),
            *by_trial.sems(),
        ],
        1,
        time_factor,
        trial_factor,
    )


def eliminate(square):
    size = square.shape[0]
    row_id = lax.broadcasted_iota(jnp.int32, (size, size), 0)
    lane_id = lax.broadcasted_iota(jnp.int32, (size, size), 1)
    lane_one = lax.broadcasted_iota(jnp.int32, (1, size), 1)
    for first in range(0, size, PANEL):
        columns = [
            jnp.broadcast_to(square[:, first + j : first + j + 1], (size, size))
            for j in range(PANEL)
        ]
        for j in range(PANEL):
            pivot = first + j
            column = columns[j]
            over = 1.0 / column[pivot : pivot + 1, :]
            row = jnp.where(lane_one == pivot, 1.0, square[pivot : pivot + 1, :]) * over
            square = jnp.where(
                row_id == pivot, row, jnp.where(lane_id == pivot, 0.0, square) - column * row
            )
            for later in range(j + 1, PANEL):
                factor = columns[later][pivot : pivot + 1, :] * over
                columns[later] = jnp.where(
                    row_id == pivot, factor, columns[later] - column * factor
                )
    return square


def inverse_kernel(gram_ref, out_ref):
    size = gram_ref.shape[0]
    half = size // 2
    gram = gram_ref[...]
    across, unused = diagonals(gram)
    mean = jnp.sum(across, axis=1, keepdims=True) / size
    on = lax.broadcasted_iota(jnp.int32, (size, size), 0) == lax.broadcasted_iota(
        jnp.int32, (size, size), 1
    )
    scaled = gram / mean + jnp.where(on, RIDGE, 0.0)
    corner = scaled[:half, half:]
    first = eliminate(scaled[:half, :half])
    carried = dot_high(first, corner)
    rest = scaled[half:, half:] - lax.dot_general(
        corner, carried, TN, precision=lax.Precision.HIGHEST, preferred_element_type=F32
    )
    second = eliminate(rest)
    mixed = dot_high(carried, second)
    out_ref[half:, half:] = second
    out_ref[:half, half:] = -mixed
    out_ref[half:, :half] = -mixed.T
    out_ref[:half, :half] = first + dot_high(mixed, carried.T)


def normal_inverse(gram):
    return pl.pallas_call(
        inverse_kernel,
        out_shape=jax.ShapeDtypeStruct(gram.shape, F32),
        in_specs=[VMEM],
        out_specs=VMEM,
        compiler_params=pltpu.CompilerParams(vmem_limit_bytes=32 << 20),
    )(gram)


def flat(blocks):
    return blocks.reshape(blocks.shape[0] * blocks.shape[1], blocks.shape[2])


def rescaled(raw, gram, total, factor_ref, other, normed_ref, product_ref):
    across, down = diagonals(gram)
    scale = jnp.sqrt(across / total + EPSILON)
    scale_down = jnp.sqrt(down / total + EPSILON)
    factor_ref[...] = (raw / scale).astype(BF16)
    normed = gram / (scale_down * scale)
    normed_ref[...] = normed
    product_ref[...] = normed * other
    return scale


def neuron_kernel(
    plane, depth, total, part, inverse, other, own_ref, local_ref, normed_ref, product_ref,
    landed, raw, grams, slices, gram, sa, sb, ra, rb, za, zb, ga, gb,
):
    meet(plane, depth)
    me = plane.me()
    layer = depth.me()
    size = gram.shape[0] * gram.shape[1]
    sums = (lambda peer: part.at[peer], lambda index: landed.at[index], (sa, sb))
    plane.send(*sums)
    plane.wait(*sums)
    raw[me] = dot_high(summed(plane, part, landed), inverse[...])
    rows = (lambda peer: raw.at[me], lambda index: raw.at[index], (ra, rb))
    plane.send(*rows)
    plane.wait(*rows)
    whole = flat(raw[...])
    grams[...] = gram_high(whole).reshape(grams.shape)
    slices[layer] = grams[me]
    level = (lambda peer: slices.at[layer], lambda index: slices.at[index], (za, zb))
    depth.send(*level)
    depth.wait(*level)
    gram[me] = jnp.sum(slices[...], axis=0)
    spread = (lambda peer: gram.at[me], lambda index: gram.at[index], (ga, gb))
    plane.send(*spread)
    plane.wait(*spread)
    scale = rescaled(
        whole, flat(gram[...]), total, local_ref, other[...], normed_ref, product_ref
    )
    own_ref[...] = (raw[me] / scale).astype(BF16)
    plane.flush(*sums)
    plane.flush(*rows)
    depth.flush(*level)
    plane.flush(*spread)


def finish_neuron(sizes, partial, inverse, other):
    plane, depth = Group(("tm", "trial"), sizes), Group(("neuron",), sizes)
    held, rank = partial.shape
    own = held // plane.count
    piece = rank // plane.count
    square = jax.ShapeDtypeStruct((rank, rank), F32)
    return call(
        functools.partial(neuron_kernel, plane, depth, held * depth.count),
        [
            jax.ShapeDtypeStruct((own, rank), BF16),
            jax.ShapeDtypeStruct((held, rank), BF16),
            square,
            square,
        ],
        [
            pltpu.VMEM((plane.count, own, rank), F32),
            pltpu.VMEM((plane.count, own, rank), F32),
            pltpu.VMEM((plane.count, piece, rank), F32),
            pltpu.VMEM((depth.count, piece, rank), F32),
            pltpu.VMEM((plane.count, piece, rank), F32),
            *plane.sems(),
            *plane.sems(),
            *depth.sems(),
            *plane.sems(),
        ],
        2,
        partial.reshape(plane.count, own, rank),
        inverse,
        other,
    )


def time_kernel(
    ring, pair, total, part, inverse, other, local_ref, normed_ref, product_ref,
    landed, raw, halves, sa, sb, ra, rb, pa, pb,
):
    meet(ring, pair)
    me = ring.me()
    side = pair.me()
    sums = (lambda peer: part.at[peer], lambda index: landed.at[index], (sa, sb))
    ring.send(*sums)
    ring.wait(*sums)
    raw[me] = dot_high(summed(ring, part, landed), inverse[...])
    rows = (lambda peer: raw.at[me], lambda index: raw.at[index], (ra, rb))
    ring.send(*rows)
    ring.wait(*rows)
    mine = flat(raw[...])
    halves[side] = mine
    swap = (lambda peer: halves.at[side], lambda index: halves.at[index], (pa, pb))
    pair.send(*swap)
    pair.wait(*swap)
    gram = gram_high(flat(halves[...]))
    unused = rescaled(mine, gram, total, local_ref, other[...], normed_ref, product_ref)
    ring.flush(*sums)
    ring.flush(*rows)
    pair.flush(*swap)


def finish_time(sizes, partial, inverse, other):
    ring, pair = Group(("neuron", "trial"), sizes), Group(("tm",), sizes)
    held, rank = partial.shape
    own = held // ring.count
    square = jax.ShapeDtypeStruct((rank, rank), F32)
    return call(
        functools.partial(time_kernel, ring, pair, held * pair.count),
        [jax.ShapeDtypeStruct((held, rank), BF16), square, square],
        [
            pltpu.VMEM((ring.count, own, rank), F32),
            pltpu.VMEM((ring.count, own, rank), F32),
            pltpu.VMEM((pair.count, held, rank), F32),
            *ring.sems(),
            *ring.sems(),
            *pair.sems(),
        ],
        3,
        partial.reshape(ring.count, own, rank),
        inverse,
        other,
    )


def trial_kernel(
    ring, everyone, total, part, inverse, local_ref, landed, raw, squares, sa, sb, ra, rb, qa, qb
):
    meet(everyone)
    me = ring.me()
    mine = everyone.me()
    sums = (lambda peer: part.at[peer], lambda index: landed.at[index], (sa, sb))
    ring.send(*sums)
    ring.wait(*sums)
    own = dot_high(summed(ring, part, landed), inverse[...])
    raw[me] = own
    squares[mine] = jnp.sum(own * own, axis=0, keepdims=True)
    rows = (lambda peer: raw.at[me], lambda index: raw.at[index], (ra, rb))
    counts = (lambda peer: squares.at[mine], lambda index: squares.at[index], (qa, qb))
    everyone.send(*counts)
    ring.send(*rows)
    everyone.wait(*counts)
    ring.wait(*rows)
    scale = jnp.sqrt(jnp.sum(squares[...], axis=0) / total + EPSILON)
    local_ref[...] = (flat(raw[...]) / scale).astype(BF16)
    ring.flush(*sums)
    ring.flush(*rows)
    everyone.flush(*counts)


def finish_trial(sizes, partial, inverse):
    ring, everyone = Group(("neuron", "tm"), sizes), Group(("neuron", "tm", "trial"), sizes)
    held, rank = partial.shape
    own = held // ring.count
    return call(
        functools.partial(trial_kernel, ring, everyone, held * sizes["trial"]),
        [jax.ShapeDtypeStruct((held, rank), BF16)],
        [
            pltpu.VMEM((ring.count, own, rank), F32),
            pltpu.VMEM((ring.count, own, rank), F32),
            pltpu.VMEM((everyone.count, 1, rank), F32),
            *ring.sems(),
            *ring.sems(),
            *everyone.sems(),
        ],
        4,
        partial.reshape(ring.count, own, rank),
        inverse,
    )[0]


def khatri_rao(left_rows, right_rows):
    return (
        left_rows.astype(jnp.float32)[:, None, :] * right_rows.astype(jnp.float32)[None, :, :]
    ).astype(jnp.bfloat16)


def mask_tensor(tensor, present_blocks, trial_day):
    day_count = present_blocks.shape[1]
    onehot = (trial_day[:, None] == jnp.arange(day_count, dtype=jnp.int32)[None, :]).astype(
        jnp.float32
    )
    block_mask = jnp.dot(present_blocks.astype(jnp.float32), onehot.T)
    block_count = present_blocks.shape[0]
    shaped = tensor.reshape(
        block_count, tensor.shape[0] // block_count, tensor.shape[1], tensor.shape[2]
    )
    return shaped * block_mask.astype(jnp.bfloat16)[:, None, None, :]


def on_device(sizes, tensor, present_blocks, trial_day, time_factor, trial_factor):
    blocks = mask_tensor(tensor, present_blocks, trial_day)
    block_count, block_rows, time_rows, trial_rows = blocks.shape
    flattened = blocks.reshape(block_count * block_rows, time_rows, trial_rows)
    rank_size = time_factor.shape[1]
    start_trial, product = start_products(sizes, time_factor, trial_factor)
    inverse_neuron = normal_inverse(product)
    kr_tk = khatri_rao(time_factor, trial_factor)
    partial = jnp.einsum("itk,tkr->ir", flattened, kr_tk, preferred_element_type=F32)
    neuron_own, neuron_local, gram_neuron, product = finish_neuron(
        sizes, partial, inverse_neuron, start_trial
    )
    inverse_time = normal_inverse(product)
    neuron_blocks = neuron_local.reshape(block_count, block_rows, rank_size)

    def time_add_block(running, inputs):
        tensor_piece, rows_a = inputs
        kr_ik = khatri_rao(rows_a, trial_factor)
        return (
            running + jnp.einsum("itk,ikr->tr", tensor_piece, kr_ik, preferred_element_type=F32),
            None,
        )

    partial, unused = lax.scan(
        time_add_block, jnp.zeros((time_rows, rank_size), F32), (blocks, neuron_blocks)
    )
    time_local, unused, product = finish_time(sizes, partial, inverse_time, gram_neuron)
    inverse_trial = normal_inverse(product)

    def trial_add_block(running, inputs):
        tensor_piece, rows_a = inputs
        kr_it = khatri_rao(rows_a, time_local)
        return (
            running + jnp.einsum("itk,itr->kr", tensor_piece, kr_it, preferred_element_type=F32),
            None,
        )

    partial, unused = lax.scan(
        trial_add_block, jnp.zeros((trial_rows, rank_size), F32), (blocks, neuron_blocks)
    )
    trial_local = finish_trial(sizes, partial, inverse_trial)
    return (neuron_own, time_local, trial_local)


def solution(mesh):
    sizes = {axis: mesh.shape[axis] for axis in mesh.axis_names}
    return jax.shard_map(
        functools.partial(on_device, sizes),
        mesh=mesh,
        in_specs=(
            P("neuron", "tm", "trial"),
            P("neuron", None),
            P("trial"),
            P("tm", None),
            P("trial", None),
        ),
        out_specs=(P(("neuron", "tm", "trial"), None), P("tm", None), P("trial", None)),
        check_vma=False,
    )
```

```python
import functools

import jax
import jax.numpy as jnp
from jax import lax
from jax.experimental import pallas as pl
from jax.experimental.pallas import tpu as pltpu
from jax.sharding import PartitionSpec as P

RIDGE = 0.1
EPSILON = 1e-06
PANEL = 4
VMEM = pl.BlockSpec(memory_space=pltpu.VMEM)
F32 = jnp.float32
BF16 = jnp.bfloat16
TN = (((0,), (0,)), ((), ()))


def dot_high(left, right):
    return jnp.dot(left, right, precision=lax.Precision.HIGHEST, preferred_element_type=F32)


def gram_high(rows):
    return lax.dot_general(
        rows, rows, TN, precision=lax.Precision.HIGHEST, preferred_element_type=F32
    )


def diagonals(square):
    size = square.shape[0]
    on = lax.broadcasted_iota(jnp.int32, (size, size), 0) == lax.broadcasted_iota(
        jnp.int32, (size, size), 1
    )
    kept = jnp.where(on, square, 0.0)
    return jnp.sum(kept, axis=0, keepdims=True), jnp.sum(kept, axis=1, keepdims=True)


class Group:
    def __init__(self, axes, sizes):
        self.axes = axes
        self.sizes = [sizes[axis] for axis in axes]
        self.count = 1
        for size in self.sizes:
            self.count *= size

    def me(self):
        index = 0
        for axis, size in zip(self.axes, self.sizes):
            index = index * size + lax.axis_index(axis)
        return index

    def where(self, index):
        place = {}
        for axis, size in reversed(list(zip(self.axes, self.sizes))):
            place[axis] = lax.rem(index, size)
            index = index // size
        return place

    def each(self, body):
        if self.count <= 32:
            for step in range(1, self.count):
                body(step)
        else:

            @pl.loop(1, self.count)
            def run(step):
                body(step)

    def greet(self, barrier):
        me = self.me()

        def body(step):
            pl.semaphore_signal(
                barrier,
                inc=1,
                device_id=self.where(lax.rem(me + step, self.count)),
                device_id_type=pl.DeviceIdType.MESH,
            )

        self.each(body)

    def copy(self, step, source, target, sems, incoming):
        me = self.me()
        peer = lax.rem(me + step, self.count)
        origin = lax.rem(me - step + self.count, self.count)
        return pltpu.make_async_remote_copy(
            src_ref=source(peer),
            dst_ref=target(origin if incoming else me),
            send_sem=sems[0].at[step],
            recv_sem=sems[1].at[step],
            device_id=self.where(peer),
            device_id_type=pl.DeviceIdType.MESH,
        )

    def send(self, source, target, sems):
        self.each(lambda step: self.copy(step, source, target, sems, False).start())

    def wait(self, source, target, sems):
        self.each(lambda step: self.copy(step, source, target, sems, True).wait_recv())

    def flush(self, source, target, sems):
        self.each(lambda step: self.copy(step, source, target, sems, False).wait_send())

    def sems(self):
        return [pltpu.SemaphoreType.DMA((self.count,)), pltpu.SemaphoreType.DMA((self.count,))]


def meet(*groups):
    barrier = pltpu.get_barrier_semaphore()
    for group in groups:
        group.greet(barrier)
    pl.semaphore_wait(barrier, sum(group.count - 1 for group in groups))


def call(body, outs, scratch, number, *operands):
    return pl.pallas_call(
        body,
        out_shape=outs,
        in_specs=[VMEM] * len(operands),
        out_specs=[VMEM] * len(outs),
        scratch_shapes=scratch,
        compiler_params=pltpu.CompilerParams(
            collective_id=number, has_side_effects=True, vmem_limit_bytes=32 << 20
        ),
    )(*operands)


def summed(group, own_ref, landed_ref):
    me = group.me()
    landed_ref[me] = own_ref[me]
    if group.count <= 32:
        total = landed_ref[0]
        for index in range(1, group.count):
            total = total + landed_ref[index]
        return total
    return lax.fori_loop(
        1, group.count, lambda index, total: total + landed_ref[index], landed_ref[0]
    )


def start_kernel(by_time, by_trial, time_ref, trial_ref, gram_ref, product_ref, times, trials, ta, tb, ra, rb):
    meet(by_time, by_trial)
    jobs = (
        (by_trial, trial_ref, trials, (ra, rb)),
        (by_time, time_ref, times, (ta, tb)),
    )
    for group, own, landed, sems in jobs:
        group.send(lambda peer: own, lambda index: landed.at[index], sems)
    for group, own, landed, sems in jobs:
        landed[group.me()] = own[...]
        group.wait(lambda peer: own, lambda index: landed.at[index], sems)
    grams = []
    for landed in (times, trials):
        count, rows, rank = landed.shape
        whole = landed[...].reshape(count * rows, rank)
        grams.append(lax.dot_general(whole, whole, TN, preferred_element_type=F32))
    gram_ref[...] = grams[1]
    product_ref[...] = grams[0] * grams[1]
    for group, own, landed, sems in jobs:
        group.flush(lambda peer: own, lambda index: landed.at[index], sems)


def start_products(sizes, time_factor, trial_factor):
    by_time, by_trial = Group(("tm",), sizes), Group(("trial",), sizes)
    rank = time_factor.shape[1]
    square = jax.ShapeDtypeStruct((rank, rank), F32)
    return call(
        functools.partial(start_kernel, by_time, by_trial),
        [square, square],
        [
            pltpu.VMEM((by_time.count, *time_factor.shape), BF16),
            pltpu.VMEM((by_trial.count, *trial_factor.shape), BF16),
            *by_time.sems(),
            *by_trial.sems(),
        ],
        1,
        time_factor,
        trial_factor,
    )


def eliminate(square):
    size = square.shape[0]
    row_id = lax.broadcasted_iota(jnp.int32, (size, size), 0)
    lane_id = lax.broadcasted_iota(jnp.int32, (size, size), 1)
    lane_one = lax.broadcasted_iota(jnp.int32, (1, size), 1)
    for first in range(0, size, PANEL):
        columns = [
            jnp.broadcast_to(square[:, first + j : first + j + 1], (size, size))
            for j in range(PANEL)
        ]
        for j in range(PANEL):
            pivot = first + j
            column = columns[j]
            over = 1.0 / column[pivot : pivot + 1, :]
            row = jnp.where(lane_one == pivot, 1.0, square[pivot : pivot + 1, :]) * over
            square = jnp.where(
                row_id == pivot, row, jnp.where(lane_id == pivot, 0.0, square) - column * row
            )
            for later in range(j + 1, PANEL):
                factor = columns[later][pivot : pivot + 1, :] * over
                columns[later] = jnp.where(
                    row_id == pivot, factor, columns[later] - column * factor
                )
    return square


def inverse_kernel(gram_ref, out_ref):
    size = gram_ref.shape[0]
    half = size // 2
    gram = gram_ref[...]
    across, unused = diagonals(gram)
    mean = jnp.sum(across, axis=1, keepdims=True) / size
    on = lax.broadcasted_iota(jnp.int32, (size, size), 0) == lax.broadcasted_iota(
        jnp.int32, (size, size), 1
    )
    scaled = gram / mean + jnp.where(on, RIDGE, 0.0)
    corner = scaled[:half, half:]
    first = eliminate(scaled[:half, :half])
    carried = dot_high(first, corner)
    rest = scaled[half:, half:] - lax.dot_general(
        corner, carried, TN, precision=lax.Precision.HIGHEST, preferred_element_type=F32
    )
    second = eliminate(rest)
    mixed = dot_high(carried, second)
    out_ref[half:, half:] = second
    out_ref[:half, half:] = -mixed
    out_ref[half:, :half] = -mixed.T
    out_ref[:half, :half] = first + dot_high(mixed, carried.T)


def normal_inverse(gram):
    return pl.pallas_call(
        inverse_kernel,
        out_shape=jax.ShapeDtypeStruct(gram.shape, F32),
        in_specs=[VMEM],
        out_specs=VMEM,
        compiler_params=pltpu.CompilerParams(vmem_limit_bytes=32 << 20),
    )(gram)


def flat(blocks):
    return blocks.reshape(blocks.shape[0] * blocks.shape[1], blocks.shape[2])


def rescaled(raw, gram, total, factor_ref, other, normed_ref, product_ref):
    across, down = diagonals(gram)
    scale = jnp.sqrt(across / total + EPSILON)
    scale_down = jnp.sqrt(down / total + EPSILON)
    factor_ref[...] = (raw / scale).astype(BF16)
    normed = gram / (scale_down * scale)
    normed_ref[...] = normed
    product_ref[...] = normed * other
    return scale


def neuron_kernel(
    plane, depth, total, part, inverse, other, own_ref, local_ref, normed_ref, product_ref,
    landed, raw, grams, slices, gram, sa, sb, ra, rb, za, zb, ga, gb,
):
    meet(plane, depth)
    me = plane.me()
    layer = depth.me()
    size = gram.shape[0] * gram.shape[1]
    sums = (lambda peer: part.at[peer], lambda index: landed.at[index], (sa, sb))
    plane.send(*sums)
    plane.wait(*sums)
    raw[me] = dot_high(summed(plane, part, landed), inverse[...])
    rows = (lambda peer: raw.at[me], lambda index: raw.at[index], (ra, rb))
    plane.send(*rows)
    plane.wait(*rows)
    whole = flat(raw[...])
    grams[...] = gram_high(whole).reshape(grams.shape)
    slices[layer] = grams[me]
    level = (lambda peer: slices.at[layer], lambda index: slices.at[index], (za, zb))
    depth.send(*level)
    depth.wait(*level)
    gram[me] = jnp.sum(slices[...], axis=0)
    spread = (lambda peer: gram.at[me], lambda index: gram.at[index], (ga, gb))
    plane.send(*spread)
    plane.wait(*spread)
    scale = rescaled(
        whole, flat(gram[...]), total, local_ref, other[...], normed_ref, product_ref
    )
    own_ref[...] = (raw[me] / scale).astype(BF16)
    plane.flush(*sums)
    plane.flush(*rows)
    depth.flush(*level)
    plane.flush(*spread)


def finish_neuron(sizes, partial, inverse, other):
    plane, depth = Group(("tm", "trial"), sizes), Group(("neuron",), sizes)
    held, rank = partial.shape
    own = held // plane.count
    piece = rank // plane.count
    square = jax.ShapeDtypeStruct((rank, rank), F32)
    return call(
        functools.partial(neuron_kernel, plane, depth, held * depth.count),
        [
            jax.ShapeDtypeStruct((own, rank), BF16),
            jax.ShapeDtypeStruct((held, rank), BF16),
            square,
            square,
        ],
        [
            pltpu.VMEM((plane.count, own, rank), F32),
            pltpu.VMEM((plane.count, own, rank), F32),
            pltpu.VMEM((plane.count, piece, rank), F32),
            pltpu.VMEM((depth.count, piece, rank), F32),
            pltpu.VMEM((plane.count, piece, rank), F32),
            *plane.sems(),
            *plane.sems(),
            *depth.sems(),
            *plane.sems(),
        ],
        2,
        partial.reshape(plane.count, own, rank),
        inverse,
        other,
    )


def time_kernel(
    ring, pair, total, part, inverse, other, local_ref, normed_ref, product_ref,
    landed, raw, halves, sa, sb, ra, rb, pa, pb,
):
    meet(ring, pair)
    me = ring.me()
    side = pair.me()
    sums = (lambda peer: part.at[peer], lambda index: landed.at[index], (sa, sb))
    ring.send(*sums)
    ring.wait(*sums)
    raw[me] = dot_high(summed(ring, part, landed), inverse[...])
    rows = (lambda peer: raw.at[me], lambda index: raw.at[index], (ra, rb))
    ring.send(*rows)
    ring.wait(*rows)
    mine = flat(raw[...])
    halves[side] = mine
    swap = (lambda peer: halves.at[side], lambda index: halves.at[index], (pa, pb))
    pair.send(*swap)
    pair.wait(*swap)
    gram = gram_high(flat(halves[...]))
    unused = rescaled(mine, gram, total, local_ref, other[...], normed_ref, product_ref)
    ring.flush(*sums)
    ring.flush(*rows)
    pair.flush(*swap)


def finish_time(sizes, partial, inverse, other):
    ring, pair = Group(("neuron", "trial"), sizes), Group(("tm",), sizes)
    held, rank = partial.shape
    own = held // ring.count
    square = jax.ShapeDtypeStruct((rank, rank), F32)
    return call(
        functools.partial(time_kernel, ring, pair, held * pair.count),
        [jax.ShapeDtypeStruct((held, rank), BF16), square, square],
        [
            pltpu.VMEM((ring.count, own, rank), F32),
            pltpu.VMEM((ring.count, own, rank), F32),
            pltpu.VMEM((pair.count, held, rank), F32),
            *ring.sems(),
            *ring.sems(),
            *pair.sems(),
        ],
        3,
        partial.reshape(ring.count, own, rank),
        inverse,
        other,
    )


def trial_kernel(
    ring, everyone, total, part, inverse, local_ref, landed, raw, squares, sa, sb, ra, rb, qa, qb
):
    meet(everyone)
    me = ring.me()
    mine = everyone.me()
    sums = (lambda peer: part.at[peer], lambda index: landed.at[index], (sa, sb))
    ring.send(*sums)
    ring.wait(*sums)
    own = dot_high(summed(ring, part, landed), inverse[...])
    raw[me] = own
    squares[mine] = jnp.sum(own * own, axis=0, keepdims=True)
    rows = (lambda peer: raw.at[me], lambda index: raw.at[index], (ra, rb))
    counts = (lambda peer: squares.at[mine], lambda index: squares.at[index], (qa, qb))
    everyone.send(*counts)
    ring.send(*rows)
    everyone.wait(*counts)
    ring.wait(*rows)
    scale = jnp.sqrt(jnp.sum(squares[...], axis=0) / total + EPSILON)
    local_ref[...] = (flat(raw[...]) / scale).astype(BF16)
    ring.flush(*sums)
    ring.flush(*rows)
    everyone.flush(*counts)


def finish_trial(sizes, partial, inverse):
    ring, everyone = Group(("neuron", "tm"), sizes), Group(("neuron", "tm", "trial"), sizes)
    held, rank = partial.shape
    own = held // ring.count
    return call(
        functools.partial(trial_kernel, ring, everyone, held * sizes["trial"]),
        [jax.ShapeDtypeStruct((held, rank), BF16)],
        [
            pltpu.VMEM((ring.count, own, rank), F32),
            pltpu.VMEM((ring.count, own, rank), F32),
            pltpu.VMEM((everyone.count, 1, rank), F32),
            *ring.sems(),
            *ring.sems(),
            *everyone.sems(),
        ],
        4,
        partial.reshape(ring.count, own, rank),
        inverse,
    )[0]


def params():
    return pltpu.CompilerParams(vmem_limit_bytes=40 << 20)


def cost(tensor, rank):
    return pl.CostEstimate(
        flops=2 * tensor.size * rank, bytes_accessed=2 * tensor.size, transcendentals=0
    )


def neuron_sums_kernel(tensor_ref, mask_ref, time_ref, trial_ref, out_ref):
    @pl.when(pl.program_id(0) == 0)
    def clear():
        out_ref[...] = jnp.zeros_like(out_ref)

    chunk = tensor_ref.shape[1]
    block_count = mask_ref.shape[0]
    block_rows = tensor_ref.shape[0] // block_count
    turned = jnp.swapaxes(tensor_ref[...], 0, 1)
    times = time_ref[...].astype(F32)
    trials = trial_ref[...].astype(F32)
    total = None
    for first in range(0, chunk, 2):
        right = jnp.concatenate(
            [(times[first + j : first + j + 1] * trials).astype(BF16) for j in range(2)], axis=0
        )
        left = jnp.concatenate(
            [
                jnp.concatenate(
                    [
                        turned[first + j, b * block_rows : (b + 1) * block_rows] * mask_ref[b]
                        for b in range(block_count)
                    ],
                    axis=0,
                )
                for j in range(2)
            ],
            axis=1,
        )
        term = jnp.dot(left, right, preferred_element_type=F32)
        total = term if total is None else total + term
    out_ref[...] += total


def neuron_sums(tensor, mask, time_factor, trial_factor):
    rows, times, trials = tensor.shape
    rank = time_factor.shape[1]
    chunk = 16
    return pl.pallas_call(
        neuron_sums_kernel,
        grid=(times // chunk,),
        in_specs=[
            pl.BlockSpec((rows, chunk, trials), lambda g: (0, g, 0)),
            pl.BlockSpec(mask.shape, lambda g: (0, 0, 0)),
            pl.BlockSpec((chunk, rank), lambda g: (g, 0)),
            pl.BlockSpec((trials, rank), lambda g: (0, 0)),
        ],
        out_specs=pl.BlockSpec((rows, rank), lambda g: (0, 0)),
        out_shape=jax.ShapeDtypeStruct((rows, rank), F32),
        cost_estimate=cost(tensor, rank),
        compiler_params=params(),
    )(tensor, mask, time_factor, trial_factor)


def time_sums_kernel(tensor_ref, rows_ref, trial_ref, out_ref):
    @pl.when(pl.program_id(0) == 0)
    def clear():
        out_ref[...] = jnp.zeros_like(out_ref)

    chunk = tensor_ref.shape[0]
    rows = rows_ref[...].astype(F32)
    trials = trial_ref[0].astype(F32)
    total = None
    for first in range(0, chunk, 2):
        right = jnp.concatenate(
            [(rows[first + j : first + j + 1] * trials).astype(BF16) for j in range(2)], axis=0
        )
        left = jnp.concatenate([tensor_ref[first], tensor_ref[first + 1]], axis=1)
        term = jnp.dot(left, right, preferred_element_type=F32)
        total = term if total is None else total + term
    out_ref[...] += total


def time_sums(tensor, masked_trials, neuron_local):
    rows, times, trials = tensor.shape
    block_count, unused, rank = masked_trials.shape
    chunk = 16
    steps = rows // block_count // chunk
    return pl.pallas_call(
        time_sums_kernel,
        grid=(rows // chunk,),
        in_specs=[
            pl.BlockSpec((chunk, times, trials), lambda g: (g, 0, 0)),
            pl.BlockSpec((chunk, rank), lambda g: (g, 0)),
            pl.BlockSpec((1, trials, rank), lambda g: (g // steps, 0, 0)),
        ],
        out_specs=pl.BlockSpec((times, rank), lambda g: (0, 0)),
        out_shape=jax.ShapeDtypeStruct((times, rank), F32),
        cost_estimate=cost(tensor, rank),
        compiler_params=params(),
    )(tensor, neuron_local, masked_trials)


def trial_sums_kernel(steps, tensor_ref, rows_ref, time_ref, mask_ref, out_ref):
    @pl.when(pl.program_id(0) == 0)
    def clear():
        out_ref[...] = jnp.zeros_like(out_ref)

    chunk = tensor_ref.shape[0]
    rows = rows_ref[...].astype(F32)
    times = time_ref[...].astype(F32)
    mask = mask_ref[0]
    total = None
    for first in range(0, chunk, 2):
        right = jnp.concatenate(
            [(rows[first + j : first + j + 1] * times).astype(BF16) for j in range(2)], axis=0
        )
        left = jnp.concatenate(
            [tensor_ref[first] * mask, tensor_ref[first + 1] * mask], axis=0
        )
        term = lax.dot_general(left, right, TN, preferred_element_type=F32)
        total = term if total is None else total + term
    out_ref[...] += total


def trial_sums(tensor, mask, neuron_local, time_local):
    rows, times, trials = tensor.shape
    rank = time_local.shape[1]
    chunk = 16
    steps = rows // mask.shape[0] // chunk
    return pl.pallas_call(
        functools.partial(trial_sums_kernel, steps),
        grid=(rows // chunk,),
        in_specs=[
            pl.BlockSpec((chunk, times, trials), lambda g: (g, 0, 0)),
            pl.BlockSpec((chunk, rank), lambda g: (g, 0)),
            pl.BlockSpec((times, rank), lambda g: (0, 0)),
            pl.BlockSpec((1, 1, trials), lambda g: (g // steps, 0, 0)),
        ],
        out_specs=pl.BlockSpec((trials, rank), lambda g: (0, 0)),
        out_shape=jax.ShapeDtypeStruct((trials, rank), F32),
        cost_estimate=cost(tensor, rank),
        compiler_params=params(),
    )(tensor, neuron_local, time_local, mask)


def block_mask(present_blocks, trial_day):
    days = jnp.arange(present_blocks.shape[1], dtype=jnp.int32)
    onehot = (trial_day[:, None] == days[None, :]).astype(F32)
    return jnp.dot(present_blocks.astype(F32), onehot.T).astype(BF16)


def on_device(sizes, tensor, present_blocks, trial_day, time_factor, trial_factor):
    flags = block_mask(present_blocks, trial_day)
    mask = flags[:, None, :]
    masked_trials = trial_factor[None, :, :] * flags[:, :, None]
    start_trial, product = start_products(sizes, time_factor, trial_factor)
    inverse_neuron = normal_inverse(product)
    partial = neuron_sums(tensor, mask, time_factor, trial_factor)
    neuron_own, neuron_local, gram_neuron, product = finish_neuron(
        sizes, partial, inverse_neuron, start_trial
    )
    inverse_time = normal_inverse(product)
    partial = time_sums(tensor, masked_trials, neuron_local)
    time_local, unused, product = finish_time(sizes, partial, inverse_time, gram_neuron)
    inverse_trial = normal_inverse(product)
    partial = trial_sums(tensor, mask, neuron_local, time_local)
    trial_local = finish_trial(sizes, partial, inverse_trial)
    return (neuron_own, time_local, trial_local)


def solution(mesh):
    sizes = {axis: mesh.shape[axis] for axis in mesh.axis_names}
    return jax.shard_map(
        functools.partial(on_device, sizes),
        mesh=mesh,
        in_specs=(
            P("neuron", "tm", "trial"),
            P("neuron", None),
            P("trial"),
            P("tm", None),
            P("trial", None),
        ),
        out_specs=(P(("neuron", "tm", "trial"), None), P("tm", None), P("trial", None)),
        check_vma=False,
    )
```
